128 devices in a mesh: blk: 16 (over y, x_hi, core), rows: 8 (over x_lo, z).
Axes of the slice: x: 4 (x_hi: 2, x_lo: 2; x = x_hi * 2 + x_lo), y: 4, z: 4, core: 2. Of those that a mesh axis runs over, the one named last changes fastest.
Arguments:
- observation_points: bfloat16 [98304, 32], P(('blk', 'rows')), may hold values from -6 to 6
- search_vectors: float32 [98304, 16], P(('blk', 'rows')), may hold values from -3 to 3
- shrinkage_levels: float32 [16], replicated, may hold values from 0.1 to 10
- holdout_group: int32 [98304, 1], P(('blk', 'rows')), may hold values from 0 to 511; in each aligned block of 768 rows (0 to 767, 768 to 1535, ...) at most 3 rows name the same one
Outputs:
- mapped_search_output: float32 [98304, 16], P(('blk', 'rows'))
- fold_curv: float32 [512, 256], P(('blk', 'rows'))
The draws below stay inside these ranges and needn't reach their ends.
Inputs may be any that keep to these rules, and one draw needn't show every extreme that they name: `holdout_group`: among the rows of one device (aligned blocks of 768 rows) no fold appears more than 3 times, and some fold appears exactly 3 times; every fold appears somewhere.
All inputs are finite; a program needn't handle non-finite values.
Results may differ from the reference program's by a relative error of at most 0.0008.
Values may be sent and summed in bfloat16 or wider, within the bound.
No kernel may reach another device: no remote copies, remote signals or barrier semaphores. Data moves between devices by JAX's collectives and lax.ppermute only.
A program may use at most 128 MiB of HBM per device.

```python
import math
import jax
import jax.numpy as jnp
import numpy as np
from jax import lax

FEATS = 32
RIDGE_COUNT = 16
FOLD_DEV = 4
SAMP_DEV = 768
SAMPLES = 98304
FOLDS = 512
SLOTS = 3


def draw_observation_points(key, part):
    key = jax.random.fold_in(key, 7)
    key_latent, key_noise = jax.random.split(key, 2)
    latent = jax.random.uniform(key_latent, (SAMPLES, 3), jnp.float32, -1.0, 1.0)
    noise = jnp.clip(0.4 * jax.random.normal(key_noise, (SAMPLES, FEATS - 3), jnp.float32), -1.6, 1.6)
    return jnp.concatenate([latent, noise], axis=1).astype(jnp.bfloat16)


def level_of(key, dims, cuts, low, top_value):
    level, own = 1.0, jax.random.fold_in(key, 6)
    for axis_at, shards_of in cuts:
        draws = jnp.exp(jax.random.uniform(jax.random.fold_in(own, axis_at), (shards_of,), jnp.float32, low / len(cuts), top_value / len(cuts)))
        level = level * jnp.repeat(draws, dims[axis_at] // shards_of).reshape([-1 if axis == axis_at else 1 for axis in range(len(dims))])
    return level


def assign_block(stream_key, own, number, rows, number_of, top, bound, lean):
    order = jax.random.permutation(stream_key, number_of)
    heavy_load, ordinary = shares(number_of, rows * top, bound, lean, True), shares(number_of, rows * top, bound, lean, False)
    places = jnp.arange(number_of)

    def named(tallies, rotation):
        used = int((tallies > 0).sum())
        fixed = max(1, used // 4)
        passed = fixed + (places - fixed + rotation * (used - fixed)) % max(1, number_of - fixed)
        return jnp.zeros((number_of,), jnp.int32).at[order[jnp.where(places < fixed, places, passed)]].set(jnp.asarray(tallies, jnp.int32))

    tallies = jnp.where(number % 4 == 0, named(heavy_load, number // 4), named(ordinary, number - number // 4 - 1))
    mixed = jax.random.permutation(jax.random.fold_in(own, 3), number_of)
    donor, receiver = mixed[0:number_of // 2 * 2:2], mixed[1:number_of // 2 * 2:2]
    room = jnp.minimum(tallies[donor] - 1, bound - tallies[receiver]) // 2
    room = jnp.where((donor == order[0]) | (receiver == order[0]) | (tallies[receiver] == 0), 0, jnp.maximum(room, 0))
    passed = jax.random.randint(jax.random.fold_in(own, 4), (number_of // 2,), 0, 1 << 20) % (room + 1)
    tallies = tallies.at[donor].add(-passed).at[receiver].add(passed)
    items = jnp.searchsorted(jnp.cumsum(tallies), jnp.arange(rows * top), side="right").astype(jnp.int32)
    grid = items.reshape(top, rows).T
    grid = grid[jax.random.permutation(jax.random.fold_in(own, 1), rows)]
    rotation = jax.random.randint(jax.random.fold_in(own, 2), (rows, 1), 0, top)
    return jnp.take_along_axis(grid, (jnp.arange(top)[None, :] + rotation) % top, axis=1)


def shares(count, total, reach, slope, full):
    portions = [(1 << 20) // math.isqrt(standing ** slope) + 1 for standing in range(1, count + 1)]
    largest = reach if full else min(reach, max(-(-total // count), total * portions[0] // sum(portions)))
    least = 1 if total - largest >= count - 1 else 0
    holding, rest = [largest] + [least] * (count - 1), total - largest - least * (count - 1)
    while rest > 0:
        free = [i for i in range(1, count) if holding[i] < largest] or [i for i in range(1, count) if holding[i] < reach]
        pool, budget = sum([portions[i] for i in free]), rest
        for i in free:
            more = min(reach - holding[i], max(1, budget * portions[i] // pool), rest)
            holding[i] = holding[i] + more
            rest = rest - more
    return np.array(holding)


def scatter_about(rng, extent, scale, reach, shards=(), dtype=jnp.bfloat16):
    drawn = jax.random.normal(rng, extent, jnp.float32) * scale
    if len(shards) > 0:
        drawn = level_of(rng, extent, shards, -0.22, 0.18) * drawn
    return jnp.clip(drawn, min=-reach, max=reach).astype(dtype)


def setup_inputs(seed: int = 0) -> dict:
    seeds = jax.random.split(jax.random.key(seed), 5)
    observation_points = draw_observation_points(jax.random.fold_in(seeds[4], 71), 0)
    search_vectors = scatter_about(seeds[1], (SAMPLES, RIDGE_COUNT), 0.5, 3.0, ((0, 128),), jnp.float32)
    shrinkage_levels = jnp.clip(jnp.exp(jax.random.uniform(seeds[2], (RIDGE_COUNT,), jnp.float32, math.log(0.1), math.log(10.0))), 0.1, 10.0)
    holdout_group_keys = jax.random.split(jax.random.fold_in(seeds[3], 1), SAMPLES // SAMP_DEV)
    holdout_group_turns = jax.random.permutation(jax.random.fold_in(seeds[3], 3), SAMPLES // SAMP_DEV)
    holdout_group = jax.vmap(lambda own, number: assign_block(jax.random.fold_in(seeds[3], 2), own, number, SAMP_DEV, FOLDS, 1, SLOTS, 2))(holdout_group_keys, holdout_group_turns).reshape((SAMPLES, 1))
    return {"observation_points": observation_points, "search_vectors": search_vectors, "shrinkage_levels": shrinkage_levels, "holdout_group": holdout_group}


kernel_rate = 0.5


def reference(observation_points, search_vectors, shrinkage_levels, holdout_group):
    half_dirs = search_vectors.astype(jnp.bfloat16)
    wide_cols = observation_points.astype(jnp.float32)
    col_norms = jnp.sum(wide_cols * wide_cols, axis=1)
    block_rows = math.gcd(SAMPLES, 512)
    query_blocks = observation_points.reshape(SAMPLES // block_rows, block_rows, FEATS)
    norm_blocks = col_norms.reshape(SAMPLES // block_rows, block_rows)

    def one_block(block_pair):
        queries, query_norms = block_pair
        inner_prod = jnp.dot(queries, observation_points.T, preferred_element_type=jnp.float32)
        distance = query_norms[:, None] + col_norms[None, :] - 2.0 * inner_prod
        weights = jnp.exp(-kernel_rate * distance).astype(jnp.bfloat16)
        return jnp.dot(weights, half_dirs, preferred_element_type=jnp.float32)

    gram_share = lax.map(one_block, (query_blocks, norm_blocks)).reshape(SAMPLES, RIDGE_COUNT)
    mapped_search_output = gram_share + shrinkage_levels[None, :] * search_vectors
    products = (search_vectors[:, :, None] * mapped_search_output[:, None, :]).reshape(SAMPLES, RIDGE_COUNT * RIDGE_COUNT)
    per_fold_sums = jax.ops.segment_sum(products, holdout_group[:, 0].astype(jnp.int32), num_segments=FOLDS)
    fold_curv = per_fold_sums * (FOLD_DEV / SAMP_DEV)
    return mapped_search_output, fold_curv
```

```python
import functools

import jax
import jax.numpy as jnp
from jax import lax
from jax.experimental import pallas as pl
from jax.experimental.pallas import tpu as pltpu
from jax.sharding import PartitionSpec as P

FOLD_DEV = 4
SLOTS = 3
LANES = 128
WIDE = 256
FEAT = 32
RIDGE = 16
FPAD = 40
CHUNK = WIDE - FPAD
ROWS = 256
LOG2E = 1.4426950408889634


def thirds(value):
    high = value.astype(jnp.bfloat16).astype(jnp.float32)
    mid = (value - high).astype(jnp.bfloat16).astype(jnp.float32)
    low = (value - high - mid).astype(jnp.bfloat16).astype(jnp.float32)
    return high, mid, low


def widened(points, ones_first):
    parts = thirds(-0.5 * jnp.sum(points * points, axis=0, keepdims=True))
    row = lax.broadcasted_iota(jnp.int32, (FPAD - FEAT, points.shape[1]), 0)
    one_at, norm_at = (0, 3) if ones_first else (3, 0)
    extra = jnp.where((row >= one_at) & (row < one_at + 3), 1.0, 0.0)
    for step, part in enumerate(parts):
        extra = jnp.where(row == norm_at + step, part, extra)
    return jnp.concatenate([points, extra], axis=0)


def apply_body(*refs):
    rows = refs[3].shape[0] // 2
    step = ROWS if (rows // ROWS) % 2 == 0 else rows // 2
    pl.run_scoped(
        functools.partial(apply_scoped, step, *refs),
        *[pltpu.ACC(unit)((step, WIDE), jnp.float32) for unit in (0, 0, 1, 1)],
    )


def apply_scoped(step, xa_ref, xb_ref, out_ref, held, feats, total, columns, *sums):
    sums = (sums[:2], sums[2:])
    blocks_a, _, span = xa_ref.shape
    blocks_b = xb_ref.shape[0]
    groups = span // LANES
    rows_a, rows_b = blocks_a * span, blocks_b * span
    passes = -(-rows_b // CHUNK)
    half = rows_a // 2
    steps = half // step
    lane = lax.broadcasted_iota(jnp.int32, (1, LANES), 1)

    def fill_a(block, carry):
        for group in range(groups):
            points = xa_ref[block, :, group * LANES : (group + 1) * LANES].astype(jnp.float32)
            rest = jnp.zeros((LANES - FPAD, LANES), jnp.float32)
            turned = jnp.concatenate([widened(points, True), rest], axis=0).T.astype(jnp.bfloat16)
            at = pl.ds(pl.multiple_of(block * span + group * LANES, LANES), LANES)
            feats[at, :] = turned
            held[at, :LANES] = turned
        return carry

    lax.fori_loop(0, blocks_a, fill_a, 0)
    held[:, LANES:] = jnp.zeros((rows_a, LANES), jnp.bfloat16)
    total[...] = jnp.zeros_like(total)
    columns[:, :LANES] = jnp.zeros((columns.shape[0], LANES), jnp.float32)
    past = columns.shape[1] - LANES - rows_b
    columns[:, LANES + rows_b :] = jnp.zeros((columns.shape[0], past), jnp.float32)

    def fill_b(block, carry):
        at = pl.ds(pl.multiple_of(LANES + block * span, LANES), span)
        panel = xb_ref[block].astype(jnp.float32)
        columns[:FPAD, at] = widened(panel[:FEAT], False)
        columns[FPAD:, at] = panel[FEAT:]
        return carry

    lax.fori_loop(0, blocks_b, fill_b, 0)

    def window(number, low, high):
        start = LANES - FPAD + number * CHUNK
        base = pl.multiple_of((start // LANES) * LANES, LANES)
        shift = start % LANES
        parts = [
            pltpu.roll(columns[low:high, pl.ds(base + k * LANES, LANES)], (LANES - shift) % LANES, 1)
            for k in range(3)
        ]
        keep = lane < LANES - shift
        return jnp.where(keep, parts[0], parts[1]), jnp.where(keep, parts[1], parts[2])

    def stage(number):
        feat_0, feat_1 = window(jnp.minimum(number, passes), 0, FPAD)
        live = jnp.where(number < passes, 1.0, 0.0)
        feat_0 = jnp.where(lane < FPAD, 0.0, feat_0) * live
        dirs_0, dirs_1 = window(jnp.maximum(number - 1, 0), FPAD, FPAD + RIDGE)
        has = jnp.where(number > 0, 1.0, 0.0)
        rest = jnp.zeros((LANES - RIDGE, LANES), jnp.float32)
        turned_0 = jnp.concatenate([dirs_0 * has, rest], axis=0).T
        turned_1 = jnp.concatenate([dirs_1 * has, rest], axis=0).T
        left = jnp.concatenate([feat_0, turned_0[FPAD:], turned_1], axis=0)
        right = jnp.concatenate([feat_1 * live, jnp.zeros((CHUNK, LANES), jnp.float32)], axis=0)
        block = jnp.concatenate([left, right], axis=1).astype(jnp.bfloat16)
        pltpu.matmul_push_rhs(block, 0, 0)
        pltpu.matmul_push_rhs(block, 0, 1)

    keep_feats = lax.broadcasted_iota(jnp.int32, (step, LANES), 1) < FPAD

    def issue(unit, number, fresh):
        at = unit * half + number * step
        pltpu.matmul_acc_lhs(sums[unit][number % 2], held[at : at + step, :], load_staged_rhs=0 if fresh else None)

    def finish(unit, number, last):
        at = unit * half + number * step
        found = pltpu.matmul_pop(sums[unit][number % 2])
        total[at : at + step, :] += found[:, :LANES]
        if not last:
            weights = jnp.exp2(found * LOG2E).astype(jnp.bfloat16)
            held[at : at + step, :LANES] = jnp.where(keep_feats, feats[at : at + step, :], weights[:, :LANES])
            held[at : at + step, LANES:] = weights[:, LANES:]

    def one_pass(more, last):
        for number in range(steps):
            for unit in range(2):
                if number + 1 < steps:
                    issue(unit, number + 1, False)
                elif more:
                    issue(unit, 0, True)
                finish(unit, number, last)

    stage(0)
    for unit in range(2):
        issue(unit, 0, True)
    stage(1)

    def middle(number, carry):
        one_pass(True, False)
        stage(number + 2)
        return carry

    lax.fori_loop(0, passes - 1, middle, 0)
    one_pass(True, False)
    one_pass(False, True)
    for block in range(blocks_a):
        for group in range(groups):
            at = block * span + group * LANES
            out_ref[block, :, group * LANES : (group + 1) * LANES] = total[at : at + LANES, :].T[:RIDGE]


def apply_kernel(rows_of, columns_of):
    blocks_a, _, span = rows_of.shape
    rows_a, rows_b = blocks_a * span, columns_of.shape[0] * span
    passes = -(-rows_b // CHUNK)
    width = LANES + -(-(passes * CHUNK + 2 * WIDE) // LANES) * LANES
    return pl.pallas_call(
        apply_body,
        out_shape=jax.ShapeDtypeStruct((blocks_a, RIDGE, span), jnp.float32),
        scratch_shapes=[
            pltpu.VMEM((rows_a, WIDE), jnp.bfloat16),
            pltpu.VMEM((rows_a, LANES), jnp.bfloat16),
            pltpu.VMEM((rows_a, LANES), jnp.float32),
            pltpu.VMEM((FPAD + RIDGE, width), jnp.float32),
        ],
        compiler_params=pltpu.CompilerParams(vmem_limit_bytes=40 * 2**20),
        cost_estimate=pl.CostEstimate(
            flops=2 * rows_a * passes * WIDE * WIDE, bytes_accessed=3 * 2**20, transcendentals=rows_a * rows_b
        ),
        name="kernel_rows",
    )(rows_of, columns_of)


def scatter_body(devices, shares_ref, dirs_ref, ridge_ref, row_ids_ref, col_ids_ref, image_ref, send_ref):
    samples = dirs_ref.shape[1]
    dirs = dirs_ref[...]
    image = jnp.sum(shares_ref[...], axis=0) + ridge_ref[...] * dirs
    row_ids = row_ids_ref[...]
    rank = jnp.zeros((1, samples), jnp.int32)
    here = lax.broadcasted_iota(jnp.int32, (LANES, samples), 1)
    for group in range(samples // LANES):
        at = slice(group * LANES, (group + 1) * LANES)
        before = lax.broadcasted_iota(jnp.int32, (LANES, samples), 0) + group * LANES < here
        same = (col_ids_ref[at, :] == row_ids) & before
        rank += jnp.sum(jnp.where(same, 1, 0), axis=0, keepdims=True)
    owner = row_ids // FOLD_DEV
    place = (row_ids % FOLD_DEV) * SLOTS + rank
    pieces = thirds(jnp.concatenate([dirs, image], axis=0))
    rest = jnp.zeros((LANES - 6 * RIDGE, samples), jnp.float32)
    stacked = jnp.concatenate([*pieces, rest], axis=0)
    filler = jnp.zeros((LANES - RIDGE, LANES), jnp.float32)
    turned = []
    for group in range(samples // LANES):
        at = slice(group * LANES, (group + 1) * LANES)
        turned.append(stacked[:, at].T)
        image_ref[at, :] = jnp.concatenate([image[:, at], filler], axis=0).T[:, :RIDGE]
    turned = jnp.concatenate(turned, axis=0).astype(jnp.bfloat16)
    device = lax.broadcasted_iota(jnp.int32, (devices, samples), 0)
    for quad in range(FOLD_DEV * SLOTS // 4):
        found = []
        for slot in range(4 * quad, 4 * quad + 4):
            chosen = jnp.where((device == owner) & (place == slot), 1.0, 0.0).astype(jnp.bfloat16)
            parts = jnp.dot(chosen, turned, preferred_element_type=jnp.float32)
            found.append(parts[:, :32] + parts[:, 32:64] + parts[:, 64:96])
        send_ref[:, quad * LANES : (quad + 1) * LANES] = jnp.concatenate(found, axis=1)


def fold_body(scale, rows_ref, out_ref):
    rows = rows_ref[...]
    products = lax.dot_general(
        rows,
        rows,
        (((0,), (0,)), ((), ())),
        precision=lax.Precision.HIGHEST,
        preferred_element_type=jnp.float32,
    )
    for fold in range(FOLD_DEV):
        found = jnp.zeros((RIDGE, RIDGE), jnp.float32)
        for slot in range(fold * SLOTS, (fold + 1) * SLOTS):
            at = 2 * RIDGE * slot
            found += products[at : at + RIDGE, at + RIDGE : at + 2 * RIDGE]
        out_ref[fold] = found * scale


def body(observation_points, search_vectors, shrinkage_levels, holdout_group):
    samples = observation_points.shape[0]
    blk_count, row_count = lax.axis_size("blk"), lax.axis_size("rows")
    devices = blk_count * row_count
    points = observation_points.T
    dirs = search_vectors.T
    panel = jnp.concatenate([points, dirs.astype(jnp.bfloat16)], axis=0)
    rows_of = lax.all_to_all(jnp.broadcast_to(points, (row_count, *points.shape)), "rows", 0, 0, tiled=True)
    columns_of = lax.all_to_all(jnp.broadcast_to(panel, (blk_count, *panel.shape)), "blk", 0, 0, tiled=True)
    shares = lax.all_to_all(apply_kernel(rows_of, columns_of), "rows", 0, 0, tiled=True)
    image, send = pl.pallas_call(
        functools.partial(scatter_body, devices),
        out_shape=[
            jax.ShapeDtypeStruct((samples, RIDGE), jnp.float32),
            jax.ShapeDtypeStruct((devices, 2 * RIDGE * FOLD_DEV * SLOTS), jnp.float32),
        ],
        compiler_params=pltpu.CompilerParams(vmem_limit_bytes=40 * 2**20),
        name="image_and_slots",
    )(shares, dirs, shrinkage_levels[:, None], holdout_group.T, holdout_group)
    received = lax.all_to_all(send, ("blk", "rows"), 0, 0, tiled=True)
    folds = pl.pallas_call(
        functools.partial(fold_body, FOLD_DEV / samples),
        out_shape=jax.ShapeDtypeStruct((FOLD_DEV, RIDGE, RIDGE), jnp.float32),
        compiler_params=pltpu.CompilerParams(vmem_limit_bytes=40 * 2**20),
        name="fold_products",
    )(received)
    return image, folds.reshape(FOLD_DEV, RIDGE * RIDGE)


def solution(mesh):
    split = P(("blk", "rows"), None)
    return jax.shard_map(
        body,
        mesh=mesh,
        in_specs=(split, split, P(), split),
        out_specs=(split, split),
        check_vma=False,
    )
```

```python
import functools

import jax
import jax.numpy as jnp
from jax import lax
from jax.experimental import pallas as pl
from jax.experimental.pallas import tpu as pltpu
from jax.sharding import PartitionSpec as P

FOLD_DEV = 4
SLOTS = 3
LANES = 128
WIDE = 256
FEAT = 32
RIDGE = 16
FPAD = 40
CHUNK = WIDE - FPAD
STEPS = 8
LOG2E = 1.4426950408889634


def thirds(value):
    high = value.astype(jnp.bfloat16).astype(jnp.float32)
    mid = (value - high).astype(jnp.bfloat16).astype(jnp.float32)
    low = (value - high - mid).astype(jnp.bfloat16).astype(jnp.float32)
    return high, mid, low


def widened(points, ones_first):
    parts = thirds(-0.5 * jnp.sum(points * points, axis=0, keepdims=True))
    row = lax.broadcasted_iota(jnp.int32, (FPAD - FEAT, points.shape[1]), 0)
    one_at, norm_at = (0, 3) if ones_first else (3, 0)
    extra = jnp.where((row >= one_at) & (row < one_at + 3), 1.0, 0.0)
    for step, part in enumerate(parts):
        extra = jnp.where(row == norm_at + step, part, extra)
    return jnp.concatenate([points, extra], axis=0)


def apply_body(*refs):
    step = refs[4].shape[0] // (2 * STEPS)
    pl.run_scoped(
        functools.partial(apply_scoped, step, *refs),
        *[pltpu.ACC(unit)((step, WIDE), jnp.float32) for unit in (0, 0, 1, 1)],
    )


def apply_scoped(step, xa_ref, xb_ref, xc_ref, out_ref, held, feats, total, columns, scale, *sums):
    sums = (sums[:2], sums[2:])
    blocks_a, _, span = xa_ref.shape
    blocks_b = xb_ref.shape[0]
    groups = span // LANES
    rows_a, rows_b = blocks_a * span, 2 * blocks_b * span
    passes = -(-rows_b // CHUNK)
    half = rows_a // 2
    steps = half // step
    lane = lax.broadcasted_iota(jnp.int32, (1, LANES), 1)

    def fill_a(block, carry):
        for group in range(groups):
            points = xa_ref[block, :, group * LANES : (group + 1) * LANES].astype(jnp.float32)
            rest = jnp.zeros((LANES - FPAD, LANES), jnp.float32)
            turned = jnp.concatenate([widened(points, True), rest], axis=0).T.astype(jnp.bfloat16)
            at = pl.ds(pl.multiple_of(block * span + group * LANES, LANES), LANES)
            feats[at, :] = turned
            held[at, :LANES] = turned
        return carry

    lax.fori_loop(0, blocks_a, fill_a, 0)
    held[:, LANES:] = jnp.zeros((rows_a, LANES), jnp.bfloat16)
    total[...] = jnp.zeros_like(total)
    columns[:, :LANES] = jnp.zeros((columns.shape[0], LANES), jnp.float32)
    past = columns.shape[1] - LANES - rows_b
    columns[:, LANES + rows_b :] = jnp.zeros((columns.shape[0], past), jnp.float32)

    def fill_b(block, carry):
        for place, ref in ((block, xb_ref), (blocks_b + block, xc_ref)):
            at = pl.ds(pl.multiple_of(LANES + place * span, LANES), span)
            panel = ref[block].astype(jnp.float32)
            columns[:FPAD, at] = widened(panel[:FEAT], False)
            columns[FPAD:, at] = panel[FEAT:]
        return carry

    lax.fori_loop(0, blocks_b, fill_b, 0)

    def window(number, low, high):
        start = LANES - FPAD + number * CHUNK
        base = pl.multiple_of((start // LANES) * LANES, LANES)
        shift = start % LANES
        parts = [
            pltpu.roll(columns[low:high, pl.ds(base + k * LANES, LANES)], (LANES - shift) % LANES, 1)
            for k in range(3)
        ]
        keep = lane < LANES - shift
        return jnp.where(keep, parts[0], parts[1]), jnp.where(keep, parts[1], parts[2])

    def stage(number):
        feat_0, feat_1 = window(jnp.minimum(number, passes), 0, FPAD)
        live = jnp.where(number < passes, 1.0, 0.0)
        feat_0 = jnp.where(lane < FPAD, 0.0, feat_0) * live
        dirs_0, dirs_1 = window(jnp.maximum(number - 1, 0), FPAD, FPAD + RIDGE)
        has = jnp.where(number > 0, 1.0, 0.0)
        rest = jnp.zeros((LANES - RIDGE, LANES), jnp.float32)
        turned_0 = jnp.concatenate([dirs_0 * has, rest], axis=0).T
        turned_1 = jnp.concatenate([dirs_1 * has, rest], axis=0).T
        left = jnp.concatenate([feat_0, turned_0[FPAD:], turned_1], axis=0)
        right = jnp.concatenate([feat_1 * live, jnp.zeros((CHUNK, LANES), jnp.float32)], axis=0)
        block = jnp.concatenate([left, right], axis=1).astype(jnp.bfloat16)
        pltpu.matmul_push_rhs(block, 0, 0)
        pltpu.matmul_push_rhs(block, 0, 1)

    scale[...] = jnp.full(scale.shape, LOG2E, jnp.float32)
    to_base_2 = scale[0:1, :]
    keep_feats = lax.broadcasted_iota(jnp.int32, (step, LANES), 1) < FPAD

    def issue(unit, number, fresh):
        at = unit * half + number * step
        pltpu.matmul_acc_lhs(sums[unit][number % 2], held[at : at + step, :], load_staged_rhs=0 if fresh else None)

    def finish(unit, number, last):
        at = unit * half + number * step
        found = pltpu.matmul_pop(sums[unit][number % 2])
        total[at : at + step, :] += found[:, :LANES]
        if not last:
            weights = jnp.exp2(found * to_base_2).astype(jnp.bfloat16)
            held[at : at + step, :LANES] = jnp.where(keep_feats, feats[at : at + step, :], weights[:, :LANES])
            held[at : at + step, LANES:] = weights[:, LANES:]

    def one_pass(more, last):
        for number in range(steps):
            for unit in range(2):
                if number + 1 < steps:
                    issue(unit, number + 1, False)
                elif more:
                    issue(unit, 0, True)
                finish(unit, number, last)

    stage(0)
    for unit in range(2):
        issue(unit, 0, True)
    stage(1)

    def middle(number, carry):
        one_pass(True, False)
        stage(number + 2)
        return carry

    lax.fori_loop(0, passes - 1, middle, 0)
    one_pass(True, False)
    one_pass(False, True)
    for block in range(blocks_a):
        for group in range(groups):
            at = block * span + group * LANES
            out_ref[block, :, group * LANES : (group + 1) * LANES] = total[at : at + LANES, :].T[:RIDGE]


def apply_kernel(rows_of, columns_of, more_columns):
    blocks_a, _, span = rows_of.shape
    rows_a, rows_b = blocks_a * span, 2 * columns_of.shape[0] * span
    passes = -(-rows_b // CHUNK)
    width = LANES + -(-(passes * CHUNK + 2 * WIDE) // LANES) * LANES
    return pl.pallas_call(
        apply_body,
        out_shape=jax.ShapeDtypeStruct((blocks_a, RIDGE, span), jnp.float32),
        scratch_shapes=[
            pltpu.VMEM((rows_a, WIDE), jnp.bfloat16),
            pltpu.VMEM((rows_a, LANES), jnp.bfloat16),
            pltpu.VMEM((rows_a, LANES), jnp.float32),
            pltpu.VMEM((FPAD + RIDGE, width), jnp.float32),
            pltpu.VMEM((8, WIDE), jnp.float32),
        ],
        compiler_params=pltpu.CompilerParams(vmem_limit_bytes=40 * 2**20),
        cost_estimate=pl.CostEstimate(
            flops=2 * rows_a * passes * WIDE * WIDE, bytes_accessed=3 * 2**20, transcendentals=rows_a * rows_b
        ),
        name="kernel_rows",
    )(rows_of, columns_of, more_columns)


def scatter_body(devices, shares_ref, dirs_ref, ridge_ref, row_ids_ref, col_ids_ref, image_ref, send_ref):
    samples = dirs_ref.shape[1]
    dirs = dirs_ref[...]
    image = jnp.sum(shares_ref[...], axis=0) + ridge_ref[...] * dirs
    image_ref[...] = image
    row_ids = row_ids_ref[...]
    rank = jnp.zeros((1, samples), jnp.int32)
    here = lax.broadcasted_iota(jnp.int32, (LANES, samples), 1)
    for group in range(samples // LANES):
        at = slice(group * LANES, (group + 1) * LANES)
        before = lax.broadcasted_iota(jnp.int32, (LANES, samples), 0) + group * LANES < here
        same = (col_ids_ref[at, :] == row_ids) & before
        rank += jnp.sum(jnp.where(same, 1, 0), axis=0, keepdims=True)
    owner = row_ids // FOLD_DEV
    place = (row_ids % FOLD_DEV) * SLOTS + rank
    pieces = thirds(jnp.concatenate([dirs, image], axis=0))
    rest = jnp.zeros((LANES - 6 * RIDGE, samples), jnp.float32)
    stacked = jnp.concatenate([*pieces, rest], axis=0)
    turned = [stacked[:, group * LANES : (group + 1) * LANES].T for group in range(samples // LANES)]
    turned = jnp.concatenate(turned, axis=0).astype(jnp.bfloat16)
    device = lax.broadcasted_iota(jnp.int32, (devices, samples), 0)
    for quad in range(FOLD_DEV * SLOTS // 4):
        found = []
        for slot in range(4 * quad, 4 * quad + 4):
            chosen = jnp.where((device == owner) & (place == slot), 1.0, 0.0).astype(jnp.bfloat16)
            parts = jnp.dot(chosen, turned, preferred_element_type=jnp.float32)
            found.append(parts[:, :32] + parts[:, 32:64] + parts[:, 64:96])
        send_ref[:, 0, quad * LANES : (quad + 1) * LANES] = jnp.concatenate(found, axis=1)


def fold_body(scale, rows_ref, out_ref):
    rows = rows_ref[:, 0, :]
    products = lax.dot_general(
        rows,
        rows,
        (((0,), (0,)), ((), ())),
        precision=lax.Precision.HIGHEST,
        preferred_element_type=jnp.float32,
    )
    for fold in range(FOLD_DEV):
        found = jnp.zeros((RIDGE, RIDGE), jnp.float32)
        for slot in range(fold * SLOTS, (fold + 1) * SLOTS):
            at = 2 * RIDGE * slot
            found += products[at : at + RIDGE, at + RIDGE : at + 2 * RIDGE]
        lines = [found[line : line + 1, :] for line in range(RIDGE)]
        out_ref[fold : fold + 1, :] = jnp.concatenate(lines, axis=1) * scale


def body(observation_points, search_vectors, shrinkage_levels, holdout_group):
    samples = observation_points.shape[0]
    blk_count, row_count = lax.axis_size("blk"), lax.axis_size("rows")
    devices = blk_count * row_count
    points = observation_points.T
    dirs = search_vectors.T
    panel = jnp.concatenate([points, dirs.astype(jnp.bfloat16)], axis=0)
    rows_of = lax.all_to_all(jnp.broadcast_to(points, (row_count, *points.shape)), "rows", 0, 0, tiled=True)
    pairs = blk_count // 2
    columns_of = lax.all_to_all(
        jnp.broadcast_to(panel, (pairs, *panel.shape)),
        "blk",
        0,
        0,
        tiled=True,
        axis_index_groups=[[2 * pair + core for pair in range(pairs)] for core in range(2)],
    )
    more_columns = lax.ppermute(columns_of, "blk", [(place, place ^ 1) for place in range(blk_count)])
    shares = lax.all_to_all(apply_kernel(rows_of, columns_of, more_columns), "rows", 0, 0, tiled=True)
    image, send = pl.pallas_call(
        functools.partial(scatter_body, devices),
        out_shape=[
            jax.ShapeDtypeStruct((RIDGE, samples), jnp.float32),
            jax.ShapeDtypeStruct((devices, 1, 2 * RIDGE * FOLD_DEV * SLOTS), jnp.float32),
        ],
        compiler_params=pltpu.CompilerParams(vmem_limit_bytes=40 * 2**20),
        name="image_and_slots",
    )(shares, dirs, shrinkage_levels[:, None], holdout_group.T, holdout_group)
    received = lax.all_to_all(send, ("blk", "rows"), 0, 0, tiled=True)
    folds = pl.pallas_call(
        functools.partial(fold_body, FOLD_DEV / samples),
        out_shape=jax.ShapeDtypeStruct((FOLD_DEV, RIDGE * RIDGE), jnp.float32),
        compiler_params=pltpu.CompilerParams(vmem_limit_bytes=40 * 2**20),
        name="fold_products",
    )(received)
    return image.T, folds


def solution(mesh):
    split = P(("blk", "rows"), None)
    return jax.shard_map(
        body,
        mesh=mesh,
        in_specs=(split, split, P(), split),
        out_specs=(split, split),
        check_vma=False,
    )
```

```python
import functools

import jax
import jax.numpy as jnp
from jax import lax
from jax.experimental import pallas as pl
from jax.experimental.pallas import tpu as pltpu
from jax.sharding import PartitionSpec as P

FOLD_DEV = 4
SLOTS = 3
SPOTS = 1024
LANES = 128
WIDE = 256
FEAT = 32
RIDGE = 16
FPAD = 40
CHUNK = WIDE - FPAD
STEPS = 8
TURNS = 2
LOG2E = 1.4426950408889634


def thirds(value):
    high = value.astype(jnp.bfloat16).astype(jnp.float32)
    mid = (value - high).astype(jnp.bfloat16).astype(jnp.float32)
    low = (value - high - mid).astype(jnp.bfloat16).astype(jnp.float32)
    return high, mid, low


def widened(points, ones_first):
    parts = thirds(-0.5 * jnp.sum(points * points, axis=0, keepdims=True))
    row = lax.broadcasted_iota(jnp.int32, (FPAD - FEAT, points.shape[1]), 0)
    one_at, norm_at = (0, 3) if ones_first else (3, 0)
    extra = jnp.where((row >= one_at) & (row < one_at + 3), 1.0, 0.0)
    for step, part in enumerate(parts):
        extra = jnp.where(row == norm_at + step, part, extra)
    return jnp.concatenate([points, extra], axis=0)


def apply_body(skip, *refs):
    step = refs[-5].shape[0] // (2 * STEPS)
    pl.run_scoped(
        functools.partial(apply_scoped, skip, step, *refs),
        *[pltpu.ACC(unit)((step, WIDE), jnp.float32) for unit in (0, 0, 1, 1)],
    )


def apply_scoped(skip, step, *refs):
    if skip:
        own_ref, before_ref, near_ref, *refs = refs
    xa_ref, xb_ref, xc_ref, out_ref, held, feats, total, columns, scale, *sums = refs
    sums = (sums[:2], sums[2:])
    blocks_a, _, span = xa_ref.shape
    blocks_b = xb_ref.shape[0] - skip
    groups = span // LANES
    rows_a, rows_b = blocks_a * span, 2 * blocks_b * span
    passes = passes_of(span, blocks_b, skip)
    half = rows_a // 2
    steps = half // step
    lane = lax.broadcasted_iota(jnp.int32, (1, LANES), 1)

    def fill_a(block, carry):
        for group in range(groups):
            points = xa_ref[block, :, group * LANES : (group + 1) * LANES].astype(jnp.float32)
            rest = jnp.zeros((LANES - FPAD, LANES), jnp.float32)
            turned = jnp.concatenate([widened(points, True), rest], axis=0).T.astype(jnp.bfloat16)
            at = pl.ds(pl.multiple_of(block * span + group * LANES, LANES), LANES)
            feats[at, :] = turned
            held[at, :LANES] = turned
        return carry

    lax.fori_loop(0, blocks_a, fill_a, 0)
    held[:, LANES:] = jnp.zeros((rows_a, LANES), jnp.bfloat16)
    total[...] = jnp.zeros_like(total)
    columns[:, :LANES] = jnp.zeros((columns.shape[0], LANES), jnp.float32)
    past = columns.shape[1] - LANES - rows_b
    columns[:, LANES + rows_b :] = jnp.zeros((columns.shape[0], past), jnp.float32)

    def fill_b(block, carry):
        for place, ref in ((block, xb_ref), (blocks_b + block, xc_ref)):
            at = pl.ds(pl.multiple_of(LANES + place * span, LANES), span)
            source = lax.rem(own_ref[0] + 1 + block, blocks_b + 1) if skip else block
            panel = ref[source].astype(jnp.float32)
            columns[:FPAD, at] = widened(panel[:FEAT], False)
            columns[FPAD:, at] = panel[FEAT:]
        return carry

    lax.fori_loop(0, blocks_b, fill_b, 0)
    if skip:
        left = 2 * span % CHUNK
        panel = near_ref[:, span - LANES :].astype(jnp.float32)
        panel = jnp.concatenate([widened(panel[:FEAT], False), panel[FEAT:]], axis=0)
        at = slice(LANES + rows_b, 2 * LANES + rows_b)
        columns[:, at] = jnp.where(lane < left, pltpu.roll(panel, left, 1), 0.0)

    def window(number, low, high):
        start = LANES - FPAD + number * CHUNK
        base = pl.multiple_of((start // LANES) * LANES, LANES)
        shift = start % LANES
        parts = [
            pltpu.roll(columns[low:high, pl.ds(base + k * LANES, LANES)], (LANES - shift) % LANES, 1)
            for k in range(3)
        ]
        keep = lane < LANES - shift
        return jnp.where(keep, parts[0], parts[1]), jnp.where(keep, parts[1], parts[2])

    def stage(number):
        feat_0, feat_1 = window(jnp.minimum(number, passes), 0, FPAD)
        live = jnp.where(number < passes, 1.0, 0.0)
        feat_0 = jnp.where(lane < FPAD, 0.0, feat_0) * live
        dirs_0, dirs_1 = window(jnp.maximum(number - 1, 0), FPAD, FPAD + RIDGE)
        has = jnp.where(number > 0, 1.0, 0.0)
        rest = jnp.zeros((LANES - RIDGE, LANES), jnp.float32)
        turned_0 = jnp.concatenate([dirs_0 * has, rest], axis=0).T
        turned_1 = jnp.concatenate([dirs_1 * has, rest], axis=0).T
        left = jnp.concatenate([feat_0, turned_0[FPAD:], turned_1], axis=0)
        right = jnp.concatenate([feat_1 * live, jnp.zeros((CHUNK, LANES), jnp.float32)], axis=0)
        block = jnp.concatenate([left, right], axis=1).astype(jnp.bfloat16)
        pltpu.matmul_push_rhs(block, 0, 0)
        pltpu.matmul_push_rhs(block, 0, 1)

    scale[...] = jnp.full(scale.shape, LOG2E, jnp.float32)
    to_base_2 = scale[0:1, :]
    keep_feats = lax.broadcasted_iota(jnp.int32, (step, LANES), 1) < FPAD

    def issue(unit, number, fresh):
        at = unit * half + number * step
        pltpu.matmul_acc_lhs(sums[unit][number % 2], held[at : at + step, :], load_staged_rhs=0 if fresh else None)

    def finish(unit, number, last):
        at = unit * half + number * step
        found = pltpu.matmul_pop(sums[unit][number % 2])
        total[at : at + step, :] += found[:, :LANES]
        if not last:
            weights = jnp.exp2(found * to_base_2).astype(jnp.bfloat16)
            held[at : at + step, :LANES] = jnp.where(keep_feats, feats[at : at + step, :], weights[:, :LANES])
            held[at : at + step, LANES:] = weights[:, LANES:]

    def one_pass(more, last):
        for number in range(steps):
            for unit in range(2):
                if number + 1 < steps:
                    issue(unit, number + 1, False)
                elif more:
                    issue(unit, 0, True)
                finish(unit, number, last)

    stage(0)
    for unit in range(2):
        issue(unit, 0, True)
    stage(1)

    def middle(trip, carry):
        for turn in range(TURNS):
            one_pass(True, False)
            stage(trip * TURNS + turn + 2)
        return carry

    trips = (passes - 1) // TURNS
    lax.fori_loop(0, trips, middle, 0)
    for number in range(trips * TURNS, passes - 1):
        one_pass(True, False)
        stage(number + 2)
    one_pass(True, False)
    one_pass(False, True)
    for block in range(blocks_a):
        for group in range(groups):
            at = block * span + group * LANES
            lanes = slice(group * LANES, (group + 1) * LANES)
            found = total[at : at + LANES, :].T[:RIDGE]
            out_ref[block, :, lanes] = found + before_ref[block, :, lanes] if skip else found


def passes_of(span, blocks_b, skip):
    if not skip:
        return 2 * blocks_b * span // CHUNK
    return -(-(2 * blocks_b * span + 2 * span % CHUNK) // CHUNK)


def apply_kernel(rows_of, columns_of, more_columns, own=None, before=None, near=None):
    skip = own is not None
    blocks_a, _, span = rows_of.shape
    blocks_b = columns_of.shape[0] - skip
    rows_a, rows_b = blocks_a * span, 2 * blocks_b * span
    passes = passes_of(span, blocks_b, skip)
    width = LANES + -(-(passes * CHUNK + 2 * WIDE) // LANES) * LANES
    whole = pl.BlockSpec(memory_space=pltpu.VMEM)
    return pl.pallas_call(
        functools.partial(apply_body, skip),
        out_shape=jax.ShapeDtypeStruct((blocks_a, RIDGE, span), jnp.float32),
        in_specs=[pl.BlockSpec(memory_space=pltpu.SMEM), whole, whole] * skip + [whole] * 3,
        scratch_shapes=[
            pltpu.VMEM((rows_a, WIDE), jnp.bfloat16),
            pltpu.VMEM((rows_a, LANES), jnp.bfloat16),
            pltpu.VMEM((rows_a, LANES), jnp.float32),
            pltpu.VMEM((FPAD + RIDGE, width), jnp.float32),
            pltpu.VMEM((8, WIDE), jnp.float32),
        ],
        compiler_params=pltpu.CompilerParams(vmem_limit_bytes=40 * 2**20),
        cost_estimate=pl.CostEstimate(
            flops=2 * rows_a * passes * WIDE * WIDE, bytes_accessed=3 * 2**20, transcendentals=rows_a * rows_b
        ),
        name="kernel_rows_rest" if skip else "kernel_rows",
    )(*([own, before, near] if skip else []), rows_of, columns_of, more_columns)


def place_body(ids_ref, dirs_ref, place_ref, copy_ref):
    ids = ids_ref[...]
    samples = ids.shape[1]
    named = ids.astype(jnp.float32)
    rank = jnp.zeros((1, samples), jnp.int32)
    here = lax.broadcasted_iota(jnp.int32, (LANES, samples), 1)
    for group in range(samples // LANES):
        at = slice(group * LANES, (group + 1) * LANES)
        turned = jnp.broadcast_to(named[:, at], (LANES, LANES)).T
        before = lax.broadcasted_iota(jnp.int32, (LANES, samples), 0) + group * LANES < here
        same = (jnp.concatenate([turned] * (samples // LANES), axis=1) == named) & before
        rank += jnp.sum(jnp.where(same, 1, 0), axis=0, keepdims=True)
    place_ref[...] = (ids // FOLD_DEV) * SPOTS + (ids % FOLD_DEV) * SLOTS + rank
    copy_ref[...] = dirs_ref[...]


def scatter_body(devices, shares_ref, dirs_ref, ridge_ref, place_ref, image_ref, send_ref):
    samples = dirs_ref.shape[1]
    dirs = dirs_ref[...]
    square = (RIDGE, RIDGE)
    diagonal = lax.broadcasted_iota(jnp.int32, square, 0) == lax.broadcasted_iota(jnp.int32, square, 1)
    ridge = jnp.sum(jnp.where(diagonal, ridge_ref[...], 0.0), axis=1, keepdims=True)
    image = jnp.sum(shares_ref[...], axis=0) + ridge * dirs
    image_ref[...] = image
    pieces = thirds(jnp.concatenate([dirs, image], axis=0))
    rest = jnp.zeros((LANES - 6 * RIDGE, samples), jnp.float32)
    stacked = jnp.concatenate([*pieces, rest], axis=0)
    turned = [stacked[:, group * LANES : (group + 1) * LANES].T for group in range(samples // LANES)]
    turned = jnp.concatenate(turned, axis=0).astype(jnp.bfloat16)
    spot = place_ref[...] - SPOTS * lax.broadcasted_iota(jnp.int32, (devices, samples), 0)
    for quad in range(FOLD_DEV * SLOTS // 4):
        found = []
        for slot in range(4 * quad, 4 * quad + 4):
            chosen = jnp.where(spot == slot, 1.0, 0.0).astype(jnp.bfloat16)
            parts = jnp.dot(chosen, turned, preferred_element_type=jnp.float32)
            found.append(parts[:, :32] + parts[:, 32:64] + parts[:, 64:96])
        send_ref[:, 0, quad * LANES : (quad + 1) * LANES] = jnp.concatenate(found, axis=1)


def fold_body(scale, rows_ref, out_ref):
    rows = rows_ref[:, 0, :]
    products = lax.dot_general(
        rows,
        rows,
        (((0,), (0,)), ((), ())),
        precision=lax.Precision.HIGHEST,
        preferred_element_type=jnp.float32,
    )
    for fold in range(FOLD_DEV):
        found = jnp.zeros((RIDGE, RIDGE), jnp.float32)
        for slot in range(fold * SLOTS, (fold + 1) * SLOTS):
            at = 2 * RIDGE * slot
            found += products[at : at + RIDGE, at + RIDGE : at + 2 * RIDGE]
        lines = [found[line : line + 1, :] for line in range(RIDGE)]
        out_ref[fold : fold + 1, :] = jnp.concatenate(lines, axis=1) * scale


def body(observation_points, search_vectors, shrinkage_levels, holdout_group):
    samples = observation_points.shape[0]
    blk_count, row_count = lax.axis_size("blk"), lax.axis_size("rows")
    devices = blk_count * row_count
    points = observation_points.T
    dirs = search_vectors.T
    panel = lax.optimization_barrier(jnp.concatenate([points, dirs.astype(jnp.bfloat16)], axis=0))
    points = panel[:FEAT]
    swap = [(place, place ^ 1) for place in range(blk_count)]
    pairs = blk_count // 2
    rows_of = lax.all_to_all(jnp.broadcast_to(points, (row_count, *points.shape)), "rows", 0, 0, tiled=True)
    partner = lax.ppermute(panel, "blk", swap)
    place, dirs = pl.pallas_call(
        place_body,
        out_shape=[
            jax.ShapeDtypeStruct((1, samples), jnp.int32),
            jax.ShapeDtypeStruct(dirs.shape, jnp.float32),
        ],
        name="places",
    )(holdout_group.T, dirs)
    to_pairs = jnp.broadcast_to(panel, (pairs, *panel.shape))
    rows_of, to_pairs, place, dirs = lax.optimization_barrier((rows_of, to_pairs, place, dirs))
    columns_of = lax.all_to_all(
        to_pairs,
        "blk",
        0,
        0,
        tiled=True,
        axis_index_groups=[[2 * pair + core for pair in range(pairs)] for core in range(2)],
    )
    near = apply_kernel(rows_of, panel[None], partner[None])
    near, columns_of = lax.optimization_barrier((near, columns_of))
    more_columns = lax.ppermute(columns_of, "blk", swap)
    own = (lax.axis_index("blk") // 2).astype(jnp.int32)[None]
    shares = apply_kernel(rows_of, columns_of, more_columns, own, near, partner)
    shares = lax.all_to_all(shares, "rows", 0, 0, tiled=True)
    image, send = pl.pallas_call(
        functools.partial(scatter_body, devices),
        out_shape=[
            jax.ShapeDtypeStruct((RIDGE, samples), jnp.float32),
            jax.ShapeDtypeStruct((devices, 1, 2 * RIDGE * FOLD_DEV * SLOTS), jnp.float32),
        ],
        compiler_params=pltpu.CompilerParams(vmem_limit_bytes=40 * 2**20),
        name="image_and_slots",
    )(shares, dirs, shrinkage_levels[None], place)
    received = lax.all_to_all(send, ("blk", "rows"), 0, 0, tiled=True)
    folds = pl.pallas_call(
        functools.partial(fold_body, FOLD_DEV / samples),
        out_shape=jax.ShapeDtypeStruct((FOLD_DEV, RIDGE * RIDGE), jnp.float32),
        compiler_params=pltpu.CompilerParams(vmem_limit_bytes=40 * 2**20),
        name="fold_products",
    )(received)
    return image.T, folds


def solution(mesh):
    split = P(("blk", "rows"), None)
    return jax.shard_map(
        body,
        mesh=mesh,
        in_specs=(split, split, P(), split),
        out_specs=(split, split),
        check_vma=False,
    )
```

```python
import functools

import jax
import jax.numpy as jnp
from jax import lax
from jax.experimental import pallas as pl
from jax.experimental.pallas import tpu as pltpu
from jax.sharding import PartitionSpec as P

FOLD_DEV = 4
SLOTS = 3
SPOTS = 1024
LANES = 128
WIDE = 256
FEAT = 32
RIDGE = 16
FPAD = 40
CHUNK = WIDE - FPAD
STEPS = 8
TURNS = 2
LOG2E = 1.4426950408889634


def thirds(value):
    high = value.astype(jnp.bfloat16).astype(jnp.float32)
    mid = (value - high).astype(jnp.bfloat16).astype(jnp.float32)
    low = (value - high - mid).astype(jnp.bfloat16).astype(jnp.float32)
    return high, mid, low


def widened(points, ones_first):
    parts = thirds(-0.5 * jnp.sum(points * points, axis=0, keepdims=True))
    row = lax.broadcasted_iota(jnp.int32, (FPAD - FEAT, points.shape[1]), 0)
    one_at, norm_at = (0, 3) if ones_first else (3, 0)
    extra = jnp.where((row >= one_at) & (row < one_at + 3), 1.0, 0.0)
    for step, part in enumerate(parts):
        extra = jnp.where(row == norm_at + step, part, extra)
    return jnp.concatenate([points, extra], axis=0)


def apply_body(skip, *refs):
    step = refs[-5].shape[0] // (2 * STEPS)
    pl.run_scoped(
        functools.partial(apply_scoped, skip, step, *refs),
        *[pltpu.ACC(unit)((step, WIDE), jnp.float32) for unit in (0, 0, 1, 1)],
    )


def apply_scoped(skip, step, *refs):
    if skip:
        own_ref, before_ref, near_ref, *refs = refs
    xa_ref, xb_ref, xc_ref, out_ref, held, feats, total, columns, scale, *sums = refs
    sums = (sums[:2], sums[2:])
    blocks_a, _, span = xa_ref.shape
    blocks_b = xb_ref.shape[0] - skip
    groups = span // LANES
    rows_a, rows_b = blocks_a * span, 2 * blocks_b * span
    passes = passes_of(span, blocks_b, skip)
    half = rows_a // 2
    steps = half // step
    lane = lax.broadcasted_iota(jnp.int32, (1, LANES), 1)

    def fill_a(block, carry):
        for group in range(groups):
            points = xa_ref[block, :, group * LANES : (group + 1) * LANES].astype(jnp.float32)
            rest = jnp.zeros((LANES - FPAD, LANES), jnp.float32)
            turned = jnp.concatenate([widened(points, True), rest], axis=0).T.astype(jnp.bfloat16)
            at = pl.ds(pl.multiple_of(block * span + group * LANES, LANES), LANES)
            feats[at, :] = turned
            held[at, :LANES] = turned
        return carry

    lax.fori_loop(0, blocks_a, fill_a, 0)
    held[:, LANES:] = jnp.zeros((rows_a, LANES), jnp.bfloat16)
    total[...] = jnp.zeros_like(total)
    columns[:, :LANES] = jnp.zeros((columns.shape[0], LANES), jnp.float32)
    past = columns.shape[1] - LANES - rows_b
    columns[:, LANES + rows_b :] = jnp.zeros((columns.shape[0], past), jnp.float32)

    def fill_b(block, carry):
        for place, ref in ((block, xb_ref), (blocks_b + block, xc_ref)):
            at = pl.ds(pl.multiple_of(LANES + place * span, LANES), span)
            source = lax.rem(own_ref[0] + 1 + block, blocks_b + 1) if skip else block
            panel = ref[source].astype(jnp.float32)
            columns[:FPAD, at] = widened(panel[:FEAT], False)
            columns[FPAD:, at] = panel[FEAT:]
        return carry

    lax.fori_loop(0, blocks_b, fill_b, 0)
    if skip:
        left = 2 * span % CHUNK
        panel = near_ref[:, span - LANES :].astype(jnp.float32)
        panel = jnp.concatenate([widened(panel[:FEAT], False), panel[FEAT:]], axis=0)
        at = slice(LANES + rows_b, 2 * LANES + rows_b)
        columns[:, at] = jnp.where(lane < left, pltpu.roll(panel, left, 1), 0.0)

    def window(number, low, high):
        start = LANES - FPAD + number * CHUNK
        base = pl.multiple_of((start // LANES) * LANES, LANES)
        shift = start % LANES
        parts = [
            pltpu.roll(columns[low:high, pl.ds(base + k * LANES, LANES)], (LANES - shift) % LANES, 1)
            for k in range(3)
        ]
        keep = lane < LANES - shift
        return jnp.where(keep, parts[0], parts[1]), jnp.where(keep, parts[1], parts[2])

    def stage(number):
        feat_0, feat_1 = window(jnp.minimum(number, passes), 0, FPAD)
        live = jnp.where(number < passes, 1.0, 0.0)
        feat_0 = jnp.where(lane < FPAD, 0.0, feat_0) * live
        dirs_0, dirs_1 = window(jnp.maximum(number - 1, 0), FPAD, FPAD + RIDGE)
        has = jnp.where(number > 0, 1.0, 0.0)
        rest = jnp.zeros((LANES - RIDGE, LANES), jnp.float32)
        turned_0 = jnp.concatenate([dirs_0 * has, rest], axis=0).T
        turned_1 = jnp.concatenate([dirs_1 * has, rest], axis=0).T
        left = jnp.concatenate([feat_0, turned_0[FPAD:], turned_1], axis=0)
        right = jnp.concatenate([feat_1 * live, jnp.zeros((CHUNK, LANES), jnp.float32)], axis=0)
        block = jnp.concatenate([left, right], axis=1).astype(jnp.bfloat16)
        pltpu.matmul_push_rhs(block, 0, 0)
        pltpu.matmul_push_rhs(block, 0, 1)

    scale[...] = jnp.full(scale.shape, LOG2E, jnp.float32)
    to_base_2 = scale[0:1, :]
    keep_feats = lax.broadcasted_iota(jnp.int32, (step, LANES), 1) < FPAD

    def issue(unit, number, fresh):
        at = unit * half + number * step
        pltpu.matmul_acc_lhs(sums[unit][number % 2], held[at : at + step, :], load_staged_rhs=0 if fresh else None)

    def finish(unit, number, last):
        at = unit * half + number * step
        found = pltpu.matmul_pop(sums[unit][number % 2])
        total[at : at + step, :] += found[:, :LANES]
        if not last:
            weights = jnp.exp2(found * to_base_2).astype(jnp.bfloat16)
            held[at : at + step, :LANES] = jnp.where(keep_feats, feats[at : at + step, :], weights[:, :LANES])
            held[at : at + step, LANES:] = weights[:, LANES:]

    def one_pass(more, last):
        for number in range(steps):
            for unit in range(2):
                if number + 1 < steps:
                    issue(unit, number + 1, False)
                elif more:
                    issue(unit, 0, True)
                finish(unit, number, last)

    stage(0)
    for unit in range(2):
        issue(unit, 0, True)
    stage(1)

    def middle(trip, carry):
        for turn in range(TURNS):
            one_pass(True, False)
            stage(trip * TURNS + turn + 2)
        return carry

    trips = (passes - 1) // TURNS
    lax.fori_loop(0, trips, middle, 0)
    for number in range(trips * TURNS, passes - 1):
        one_pass(True, False)
        stage(number + 2)
    one_pass(True, False)
    one_pass(False, True)
    for block in range(blocks_a):
        for group in range(groups):
            at = block * span + group * LANES
            lanes = slice(group * LANES, (group + 1) * LANES)
            found = total[at : at + LANES, :].T[:RIDGE]
            out_ref[block, :, lanes] = found + before_ref[block, :, lanes] if skip else found


def passes_of(span, blocks_b, skip):
    if not skip:
        return 2 * blocks_b * span // CHUNK
    return -(-(2 * blocks_b * span + 2 * span % CHUNK) // CHUNK)


def apply_kernel(rows_of, columns_of, more_columns, own=None, before=None, near=None):
    skip = own is not None
    blocks_a, _, span = rows_of.shape
    blocks_b = columns_of.shape[0] - skip
    rows_a, rows_b = blocks_a * span, 2 * blocks_b * span
    passes = passes_of(span, blocks_b, skip)
    width = LANES + -(-(passes * CHUNK + 2 * WIDE) // LANES) * LANES
    whole = pl.BlockSpec(memory_space=pltpu.VMEM)
    return pl.pallas_call(
        functools.partial(apply_body, skip),
        out_shape=jax.ShapeDtypeStruct((blocks_a, RIDGE, span), jnp.float32),
        in_specs=[pl.BlockSpec(memory_space=pltpu.SMEM), whole, whole] * skip + [whole] * 3,
        scratch_shapes=[
            pltpu.VMEM((rows_a, WIDE), jnp.bfloat16),
            pltpu.VMEM((rows_a, LANES), jnp.bfloat16),
            pltpu.VMEM((rows_a, LANES), jnp.float32),
            pltpu.VMEM((FPAD + RIDGE, width), jnp.float32),
            pltpu.VMEM((8, WIDE), jnp.float32),
        ],
        compiler_params=pltpu.CompilerParams(vmem_limit_bytes=40 * 2**20),
        cost_estimate=pl.CostEstimate(
            flops=2 * rows_a * passes * WIDE * WIDE, bytes_accessed=3 * 2**20, transcendentals=rows_a * rows_b
        ),
        name="kernel_rows_rest" if skip else "kernel_rows",
    )(*([own, before, near] if skip else []), rows_of, columns_of, more_columns)


def panel_body(points_ref, dirs_ref, panel_ref, to_rows_ref):
    points = points_ref[...]
    panel_ref[...] = jnp.concatenate([points, dirs_ref[...].astype(jnp.bfloat16)], axis=0)
    for device in range(to_rows_ref.shape[0]):
        to_rows_ref[device] = points


def place_body(ids_ref, dirs_ref, ridge_ref, panel_ref, place_ref, copy_ref, ridged_ref, own_ref, to_pairs_ref):
    ids = ids_ref[...]
    samples = ids.shape[1]
    named = ids.astype(jnp.float32)
    rank = jnp.zeros((1, samples), jnp.int32)
    here = lax.broadcasted_iota(jnp.int32, (LANES, samples), 1)
    for group in range(samples // LANES):
        at = slice(group * LANES, (group + 1) * LANES)
        turned = jnp.broadcast_to(named[:, at], (LANES, LANES)).T
        before = lax.broadcasted_iota(jnp.int32, (LANES, samples), 0) + group * LANES < here
        same = (jnp.concatenate([turned] * (samples // LANES), axis=1) == named) & before
        rank += jnp.sum(jnp.where(same, 1, 0), axis=0, keepdims=True)
    place_ref[...] = (ids // FOLD_DEV) * SPOTS + (ids % FOLD_DEV) * SLOTS + rank
    dirs = dirs_ref[...]
    square = (RIDGE, RIDGE)
    diagonal = lax.broadcasted_iota(jnp.int32, square, 0) == lax.broadcasted_iota(jnp.int32, square, 1)
    copy_ref[...] = dirs
    ridged_ref[...] = jnp.sum(jnp.where(diagonal, ridge_ref[...], 0.0), axis=1, keepdims=True) * dirs
    own_ref[0] = panel_ref[...]
    for device in range(to_pairs_ref.shape[0]):
        to_pairs_ref[device] = panel_ref[...]


def scatter_body(devices, shares_ref, dirs_ref, ridged_ref, place_ref, image_ref, send_ref):
    samples = dirs_ref.shape[1]
    dirs = dirs_ref[...]
    image = jnp.sum(shares_ref[...], axis=0) + ridged_ref[...]
    image_ref[...] = image
    pieces = thirds(jnp.concatenate([dirs, image], axis=0))
    rest = jnp.zeros((LANES - 6 * RIDGE, samples), jnp.float32)
    stacked = jnp.concatenate([*pieces, rest], axis=0)
    turned = [stacked[:, group * LANES : (group + 1) * LANES].T for group in range(samples // LANES)]
    turned = jnp.concatenate(turned, axis=0).astype(jnp.bfloat16)
    spot = place_ref[...] - SPOTS * lax.broadcasted_iota(jnp.int32, (devices, samples), 0)
    for quad in range(FOLD_DEV * SLOTS // 4):
        found = []
        for slot in range(4 * quad, 4 * quad + 4):
            chosen = jnp.where(spot == slot, 1.0, 0.0).astype(jnp.bfloat16)
            parts = jnp.dot(chosen, turned, preferred_element_type=jnp.float32)
            found.append(parts[:, :32] + parts[:, 32:64] + parts[:, 64:96])
        send_ref[:, 0, quad * LANES : (quad + 1) * LANES] = jnp.concatenate(found, axis=1)


def fold_body(scale, rows_ref, out_ref):
    rows = rows_ref[:, 0, :]
    products = lax.dot_general(
        rows,
        rows,
        (((0,), (0,)), ((), ())),
        precision=lax.Precision.HIGHEST,
        preferred_element_type=jnp.float32,
    )
    for fold in range(FOLD_DEV):
        found = jnp.zeros((RIDGE, RIDGE), jnp.float32)
        for slot in range(fold * SLOTS, (fold + 1) * SLOTS):
            at = 2 * RIDGE * slot
            found += products[at : at + RIDGE, at + RIDGE : at + 2 * RIDGE]
        lines = [found[line : line + 1, :] for line in range(RIDGE)]
        out_ref[fold : fold + 1, :] = jnp.concatenate(lines, axis=1) * scale


def body(observation_points, search_vectors, shrinkage_levels, holdout_group):
    samples = observation_points.shape[0]
    blk_count, row_count = lax.axis_size("blk"), lax.axis_size("rows")
    devices = blk_count * row_count
    pairs = blk_count // 2
    swap = [(place, place ^ 1) for place in range(blk_count)]
    dirs = search_vectors.T
    panel, to_rows = pl.pallas_call(
        panel_body,
        out_shape=[
            jax.ShapeDtypeStruct((FEAT + RIDGE, samples), jnp.bfloat16),
            jax.ShapeDtypeStruct((row_count, FEAT, samples), jnp.bfloat16),
        ],
        name="panels",
    )(observation_points.T, dirs)
    rows_of = lax.all_to_all(to_rows, "rows", 0, 0, tiled=True)
    partner = lax.ppermute(panel, "blk", swap)
    place, dirs, ridged, own_panel, to_pairs = pl.pallas_call(
        place_body,
        out_shape=[
            pltpu.VMEM((1, samples), jnp.int32),
            pltpu.VMEM(dirs.shape, jnp.float32),
            pltpu.VMEM(dirs.shape, jnp.float32),
            pltpu.VMEM((1, *panel.shape), jnp.bfloat16),
            jax.ShapeDtypeStruct((pairs, *panel.shape), jnp.bfloat16),
        ],
        name="places",
    )(holdout_group.T, dirs, shrinkage_levels[None], panel)
    rows_of, to_pairs, own_panel, place, dirs, ridged = lax.optimization_barrier(
        (rows_of, to_pairs, own_panel, place, dirs, ridged)
    )
    columns_of = lax.all_to_all(
        to_pairs,
        "blk",
        0,
        0,
        tiled=True,
        axis_index_groups=[[2 * pair + core for pair in range(pairs)] for core in range(2)],
    )
    near = apply_kernel(rows_of, own_panel, partner[None])
    near, columns_of = lax.optimization_barrier((near, columns_of))
    more_columns = lax.ppermute(columns_of, "blk", swap)
    own = (lax.axis_index("blk") // 2).astype(jnp.int32)[None]
    shares = apply_kernel(rows_of, columns_of, more_columns, own, near, partner)
    shares = lax.all_to_all(shares, "rows", 0, 0, tiled=True)
    image, send = pl.pallas_call(
        functools.partial(scatter_body, devices),
        out_shape=[
            jax.ShapeDtypeStruct((RIDGE, samples), jnp.float32),
            jax.ShapeDtypeStruct((devices, 1, 2 * RIDGE * FOLD_DEV * SLOTS), jnp.float32),
        ],
        compiler_params=pltpu.CompilerParams(vmem_limit_bytes=40 * 2**20),
        name="image_and_slots",
    )(shares, dirs, ridged, place)
    received = lax.all_to_all(send, ("blk", "rows"), 0, 0, tiled=True)
    folds = pl.pallas_call(
        functools.partial(fold_body, FOLD_DEV / samples),
        out_shape=jax.ShapeDtypeStruct((FOLD_DEV, RIDGE * RIDGE), jnp.float32),
        compiler_params=pltpu.CompilerParams(vmem_limit_bytes=40 * 2**20),
        name="fold_products",
    )(received)
    return image.T, folds


def solution(mesh):
    split = P(("blk", "rows"), None)
    return jax.shard_map(
        body,
        mesh=mesh,
        in_specs=(split, split, P(), split),
        out_specs=(split, split),
        check_vma=False,
    )
```

```python
import functools

import jax
import jax.numpy as jnp
from jax import lax
from jax.experimental import pallas as pl
from jax.experimental.pallas import tpu as pltpu
from jax.sharding import PartitionSpec as P

FOLD_DEV = 4
SLOTS = 3
SPOTS = 1024
LANES = 128
WIDE = 256
FEAT = 32
RIDGE = 16
FPAD = 40
CHUNK = WIDE - FPAD
STEPS = 8
TURNS = 2
LOG2E = 1.4426950408889634


def thirds(value):
    high = value.astype(jnp.bfloat16).astype(jnp.float32)
    mid = (value - high).astype(jnp.bfloat16).astype(jnp.float32)
    low = (value - high - mid).astype(jnp.bfloat16).astype(jnp.float32)
    return high, mid, low


def widened(points, ones_first):
    parts = thirds(-0.5 * jnp.sum(points * points, axis=0, keepdims=True))
    row = lax.broadcasted_iota(jnp.int32, (FPAD - FEAT, points.shape[1]), 0)
    one_at, norm_at = (0, 3) if ones_first else (3, 0)
    extra = jnp.where((row >= one_at) & (row < one_at + 3), 1.0, 0.0)
    for step, part in enumerate(parts):
        extra = jnp.where(row == norm_at + step, part, extra)
    return jnp.concatenate([points, extra], axis=0)


def apply_body(skip, *refs):
    step = refs[-5].shape[0] // (2 * STEPS)
    pl.run_scoped(
        functools.partial(apply_scoped, skip, step, *refs),
        *[pltpu.ACC(unit)((step, WIDE), jnp.float32) for unit in (0, 0, 1, 1)],
    )


def apply_scoped(skip, step, *refs):
    if skip:
        own_ref, before_ref, near_ref, *refs = refs
    xa_ref, xb_ref, xc_ref, out_ref, held, feats, total, columns, scale, *sums = refs
    sums = (sums[:2], sums[2:])
    blocks_a, _, span = xa_ref.shape
    blocks_b = xb_ref.shape[0] - skip
    groups = span // LANES
    rows_a, rows_b = blocks_a * span, 2 * blocks_b * span
    passes = passes_of(span, blocks_b, skip)
    half = rows_a // 2
    steps = half // step
    lane = lax.broadcasted_iota(jnp.int32, (1, LANES), 1)

    def fill_a(block, carry):
        for group in range(groups):
            points = xa_ref[block, :, group * LANES : (group + 1) * LANES].astype(jnp.float32)
            rest = jnp.zeros((LANES - FPAD, LANES), jnp.float32)
            turned = jnp.concatenate([widened(points, True), rest], axis=0).T.astype(jnp.bfloat16)
            at = pl.ds(pl.multiple_of(block * span + group * LANES, LANES), LANES)
            feats[at, :] = turned
            held[at, :LANES] = turned
            held[at, LANES:] = jnp.zeros((LANES, LANES), jnp.bfloat16)
            total[at, :] = jnp.zeros((LANES, LANES), jnp.float32)
        return carry

    lax.fori_loop(0, blocks_a, fill_a, 0)
    columns[:, :LANES] = jnp.zeros((columns.shape[0], LANES), jnp.float32)
    past = columns.shape[1] - LANES - rows_b
    columns[:, LANES + rows_b :] = jnp.zeros((columns.shape[0], past), jnp.float32)

    def fill_b(block, carry):
        for place, ref in ((block, xb_ref), (blocks_b + block, xc_ref)):
            at = pl.ds(pl.multiple_of(LANES + place * span, LANES), span)
            source = lax.rem(own_ref[0] + 1 + block, blocks_b + 1) if skip else block
            panel = ref[source].astype(jnp.float32)
            columns[:FPAD, at] = widened(panel[:FEAT], False)
            columns[FPAD:, at] = panel[FEAT:]
        return carry

    lax.fori_loop(0, blocks_b, fill_b, 0)
    if skip:
        left = 2 * span % CHUNK
        panel = near_ref[:, span - LANES :].astype(jnp.float32)
        panel = jnp.concatenate([widened(panel[:FEAT], False), panel[FEAT:]], axis=0)
        at = slice(LANES + rows_b, 2 * LANES + rows_b)
        columns[:, at] = jnp.where(lane < left, pltpu.roll(panel, left, 1), 0.0)

    def window(number, low, high):
        start = LANES - FPAD + number * CHUNK
        base = pl.multiple_of((start // LANES) * LANES, LANES)
        shift = start % LANES
        parts = [
            pltpu.roll(columns[low:high, pl.ds(base + k * LANES, LANES)], (LANES - shift) % LANES, 1)
            for k in range(3)
        ]
        keep = lane < LANES - shift
        return jnp.where(keep, parts[0], parts[1]), jnp.where(keep, parts[1], parts[2])

    def stage(number):
        feat_0, feat_1 = window(jnp.minimum(number, passes), 0, FPAD)
        live = jnp.where(number < passes, 1.0, 0.0)
        feat_0 = jnp.where(lane < FPAD, 0.0, feat_0) * live
        dirs_0, dirs_1 = window(jnp.maximum(number - 1, 0), FPAD, FPAD + RIDGE)
        has = jnp.where(number > 0, 1.0, 0.0)
        rest = jnp.zeros((LANES - RIDGE, LANES), jnp.float32)
        turned_0 = jnp.concatenate([dirs_0 * has, rest], axis=0).T
        turned_1 = jnp.concatenate([dirs_1 * has, rest], axis=0).T
        left = jnp.concatenate([feat_0, turned_0[FPAD:], turned_1], axis=0)
        right = jnp.concatenate([feat_1 * live, jnp.zeros((CHUNK, LANES), jnp.float32)], axis=0)
        block = jnp.concatenate([left, right], axis=1).astype(jnp.bfloat16)
        pltpu.matmul_push_rhs(block, 0, 0)
        pltpu.matmul_push_rhs(block, 0, 1)

    scale[...] = jnp.full(scale.shape, LOG2E, jnp.float32)
    to_base_2 = scale[0:1, :]
    keep_feats = lax.broadcasted_iota(jnp.int32, (step, LANES), 1) < FPAD

    def issue(unit, number, fresh):
        at = unit * half + number * step
        pltpu.matmul_acc_lhs(sums[unit][number % 2], held[at : at + step, :], load_staged_rhs=0 if fresh else None)

    def finish(unit, number, last):
        at = unit * half + number * step
        found = pltpu.matmul_pop(sums[unit][number % 2])
        total[at : at + step, :] += found[:, :LANES]
        if not last:
            weights = jnp.exp2(found * to_base_2).astype(jnp.bfloat16)
            held[at : at + step, :LANES] = jnp.where(keep_feats, feats[at : at + step, :], weights[:, :LANES])
            held[at : at + step, LANES:] = weights[:, LANES:]

    def one_pass(more, last):
        for number in range(steps):
            for unit in range(2):
                if number + 1 < steps:
                    issue(unit, number + 1, False)
                elif more:
                    issue(unit, 0, True)
                finish(unit, number, last)

    stage(0)
    for unit in range(2):
        issue(unit, 0, True)
    stage(1)

    def middle(trip, carry):
        for turn in range(TURNS):
            one_pass(True, False)
            stage(trip * TURNS + turn + 2)
        return carry

    trips = (passes - 1) // TURNS
    lax.fori_loop(0, trips, middle, 0)
    for number in range(trips * TURNS, passes - 1):
        one_pass(True, False)
        stage(number + 2)
    one_pass(True, False)
    one_pass(False, True)
    for block in range(blocks_a):
        for group in range(groups):
            at = block * span + group * LANES
            lanes = slice(group * LANES, (group + 1) * LANES)
            found = total[at : at + LANES, :].T[:RIDGE]
            out_ref[block, :, lanes] = found + before_ref[block, :, lanes] if skip else found


def passes_of(span, blocks_b, skip):
    if not skip:
        return 2 * blocks_b * span // CHUNK
    return -(-(2 * blocks_b * span + 2 * span % CHUNK) // CHUNK)


def apply_kernel(rows_of, columns_of, more_columns, own=None, before=None, near=None):
    skip = own is not None
    blocks_a, _, span = rows_of.shape
    blocks_b = columns_of.shape[0] - skip
    rows_a, rows_b = blocks_a * span, 2 * blocks_b * span
    passes = passes_of(span, blocks_b, skip)
    width = LANES + -(-(passes * CHUNK + 2 * WIDE) // LANES) * LANES
    whole = pl.BlockSpec(memory_space=pltpu.VMEM)
    return pl.pallas_call(
        functools.partial(apply_body, skip),
        out_shape=jax.ShapeDtypeStruct((blocks_a, RIDGE, span), jnp.float32),
        in_specs=[pl.BlockSpec(memory_space=pltpu.SMEM), whole, whole] * skip + [whole] * 3,
        scratch_shapes=[
            pltpu.VMEM((rows_a, WIDE), jnp.bfloat16),
            pltpu.VMEM((rows_a, LANES), jnp.bfloat16),
            pltpu.VMEM((rows_a, LANES), jnp.float32),
            pltpu.VMEM((FPAD + RIDGE, width), jnp.float32),
            pltpu.VMEM((8, WIDE), jnp.float32),
        ],
        compiler_params=pltpu.CompilerParams(vmem_limit_bytes=40 * 2**20),
        cost_estimate=pl.CostEstimate(
            flops=2 * rows_a * passes * WIDE * WIDE, bytes_accessed=3 * 2**20, transcendentals=rows_a * rows_b
        ),
        name="kernel_rows_rest" if skip else "kernel_rows",
    )(*([own, before, near] if skip else []), rows_of, columns_of, more_columns)


def panel_body(points_ref, dirs_ref, panel_ref, to_rows_ref):
    points = points_ref[...]
    panel_ref[...] = jnp.concatenate([points, dirs_ref[...].astype(jnp.bfloat16)], axis=0)
    for device in range(to_rows_ref.shape[0]):
        to_rows_ref[device] = points


def place_body(ids_ref, dirs_ref, ridge_ref, panel_ref, place_ref, copy_ref, ridged_ref, own_ref, to_pairs_ref):
    ids = ids_ref[...]
    samples = ids.shape[1]
    named = ids.astype(jnp.float32)
    rank = jnp.zeros((1, samples), jnp.int32)
    here = lax.broadcasted_iota(jnp.int32, (LANES, samples), 1)
    for group in range(samples // LANES):
        at = slice(group * LANES, (group + 1) * LANES)
        turned = jnp.broadcast_to(named[:, at], (LANES, LANES)).T
        before = lax.broadcasted_iota(jnp.int32, (LANES, samples), 0) + group * LANES < here
        same = (jnp.concatenate([turned] * (samples // LANES), axis=1) == named) & before
        rank += jnp.sum(jnp.where(same, 1, 0), axis=0, keepdims=True)
    place_ref[...] = (ids // FOLD_DEV) * SPOTS + (ids % FOLD_DEV) * SLOTS + rank
    dirs = dirs_ref[...]
    square = (RIDGE, RIDGE)
    diagonal = lax.broadcasted_iota(jnp.int32, square, 0) == lax.broadcasted_iota(jnp.int32, square, 1)
    copy_ref[...] = dirs
    ridged_ref[...] = jnp.sum(jnp.where(diagonal, ridge_ref[...], 0.0), axis=1, keepdims=True) * dirs
    own_ref[0] = panel_ref[...]
    for device in range(to_pairs_ref.shape[0]):
        to_pairs_ref[device] = panel_ref[...]


def scatter_body(devices, shares_ref, dirs_ref, ridged_ref, place_ref, image_ref, send_ref):
    samples = dirs_ref.shape[1]
    dirs = dirs_ref[...]
    image = jnp.sum(shares_ref[...], axis=0) + ridged_ref[...]
    image_ref[...] = image
    pieces = thirds(jnp.concatenate([dirs, image], axis=0))
    rest = jnp.zeros((LANES - 6 * RIDGE, samples), jnp.float32)
    stacked = jnp.concatenate([*pieces, rest], axis=0)
    turned = [stacked[:, group * LANES : (group + 1) * LANES].T for group in range(samples // LANES)]
    turned = jnp.concatenate(turned, axis=0).astype(jnp.bfloat16)
    spot = place_ref[...] - SPOTS * lax.broadcasted_iota(jnp.int32, (devices, samples), 0)
    for quad in range(FOLD_DEV * SLOTS // 4):
        found = []
        for slot in range(4 * quad, 4 * quad + 4):
            chosen = jnp.where(spot == slot, 1.0, 0.0).astype(jnp.bfloat16)
            parts = jnp.dot(chosen, turned, preferred_element_type=jnp.float32)
            found.append(parts[:, :32] + parts[:, 32:64] + parts[:, 64:96])
        send_ref[:, 0, quad * LANES : (quad + 1) * LANES] = jnp.concatenate(found, axis=1)


def fold_body(scale, rows_ref, out_ref):
    rows = rows_ref[:, 0, :]
    width = 2 * RIDGE
    turned = rows.T
    dirs = jnp.concatenate([turned[at : at + RIDGE] for at in range(0, turned.shape[0], width)], axis=0)
    products = jnp.dot(dirs, rows, precision=lax.Precision.HIGHEST, preferred_element_type=jnp.float32)
    for fold in range(FOLD_DEV):
        found = jnp.zeros((RIDGE, RIDGE), jnp.float32)
        for slot in range(fold * SLOTS, (fold + 1) * SLOTS):
            at = width * slot + RIDGE
            found += products[slot * RIDGE : (slot + 1) * RIDGE, at : at + RIDGE]
        lines = [found[line : line + 1, :] for line in range(RIDGE)]
        out_ref[fold : fold + 1, :] = jnp.concatenate(lines, axis=1) * scale


def body(observation_points, search_vectors, shrinkage_levels, holdout_group):
    samples = observation_points.shape[0]
    blk_count, row_count = lax.axis_size("blk"), lax.axis_size("rows")
    devices = blk_count * row_count
    pairs = blk_count // 2
    swap = [(place, place ^ 1) for place in range(blk_count)]
    dirs = search_vectors.T
    panel, to_rows = pl.pallas_call(
        panel_body,
        out_shape=[
            jax.ShapeDtypeStruct((FEAT + RIDGE, samples), jnp.bfloat16),
            jax.ShapeDtypeStruct((row_count, FEAT, samples), jnp.bfloat16),
        ],
        name="panels",
    )(observation_points.T, dirs)
    rows_of = lax.all_to_all(to_rows, "rows", 0, 0, tiled=True)
    partner = lax.ppermute(panel, "blk", swap)
    place, dirs, ridged, own_panel, to_pairs = pl.pallas_call(
        place_body,
        out_shape=[
            pltpu.VMEM((1, samples), jnp.int32),
            pltpu.VMEM(dirs.shape, jnp.float32),
            pltpu.VMEM(dirs.shape, jnp.float32),
            pltpu.VMEM((1, *panel.shape), jnp.bfloat16),
            jax.ShapeDtypeStruct((pairs, *panel.shape), jnp.bfloat16),
        ],
        name="places",
    )(holdout_group.T, dirs, shrinkage_levels[None], panel)
    rows_of, to_pairs, own_panel, place, dirs, ridged = lax.optimization_barrier(
        (rows_of, to_pairs, own_panel, place, dirs, ridged)
    )
    columns_of = lax.all_to_all(
        to_pairs,
        "blk",
        0,
        0,
        tiled=True,
        axis_index_groups=[[2 * pair + core for pair in range(pairs)] for core in range(2)],
    )
    near = apply_kernel(rows_of, own_panel, partner[None])
    near, columns_of = lax.optimization_barrier((near, columns_of))
    more_columns = lax.ppermute(columns_of, "blk", swap)
    own = (lax.axis_index("blk") // 2).astype(jnp.int32)[None]
    shares = apply_kernel(rows_of, columns_of, more_columns, own, near, partner)
    shares = lax.all_to_all(shares, "rows", 0, 0, tiled=True)
    image, send = pl.pallas_call(
        functools.partial(scatter_body, devices),
        out_shape=[
            jax.ShapeDtypeStruct((RIDGE, samples), jnp.float32),
            jax.ShapeDtypeStruct((devices, 1, 2 * RIDGE * FOLD_DEV * SLOTS), jnp.float32),
        ],
        compiler_params=pltpu.CompilerParams(vmem_limit_bytes=40 * 2**20),
        name="image_and_slots",
    )(shares, dirs, ridged, place)
    received = lax.all_to_all(send, ("blk", "rows"), 0, 0, tiled=True)
    folds = pl.pallas_call(
        functools.partial(fold_body, FOLD_DEV / samples),
        out_shape=jax.ShapeDtypeStruct((FOLD_DEV, RIDGE * RIDGE), jnp.float32),
        compiler_params=pltpu.CompilerParams(vmem_limit_bytes=40 * 2**20),
        name="fold_products",
    )(received)
    return image.T, folds


def solution(mesh):
    split = P(("blk", "rows"), None)
    return jax.shard_map(
        body,
        mesh=mesh,
        in_specs=(split, split, P(), split),
        out_specs=(split, split),
        check_vma=False,
    )
```

```python
import functools

import jax
import jax.numpy as jnp
from jax import lax
from jax.experimental import pallas as pl
from jax.experimental.pallas import tpu as pltpu
from jax.sharding import PartitionSpec as P

FOLD_DEV = 4
SLOTS = 3
SPOTS = 1024
LANES = 128
WIDE = 256
FEAT = 32
RIDGE = 16
FPAD = 40
CHUNK = WIDE - FPAD
STEPS = 8
TURNS = 2
LOG2E = 1.4426950408889634


def thirds(value):
    high = value.astype(jnp.bfloat16).astype(jnp.float32)
    mid = (value - high).astype(jnp.bfloat16).astype(jnp.float32)
    low = (value - high - mid).astype(jnp.bfloat16).astype(jnp.float32)
    return high, mid, low


def widened(points, ones_first):
    parts = thirds(-0.5 * jnp.sum(points * points, axis=0, keepdims=True))
    row = lax.broadcasted_iota(jnp.int32, (FPAD - FEAT, points.shape[1]), 0)
    one_at, norm_at = (0, 3) if ones_first else (3, 0)
    extra = jnp.where((row >= one_at) & (row < one_at + 3), 1.0, 0.0)
    for step, part in enumerate(parts):
        extra = jnp.where(row == norm_at + step, part, extra)
    return jnp.concatenate([points, extra], axis=0)


def apply_body(skip, *refs):
    step = refs[-5].shape[0] // (2 * STEPS)
    pl.run_scoped(
        functools.partial(apply_scoped, skip, step, *refs),
        *[pltpu.ACC(unit)((step, WIDE), jnp.float32) for unit in (0, 0, 1, 1)],
    )


def apply_scoped(skip, step, *refs):
    if skip:
        own_ref, before_ref, near_ref, *refs = refs
    xa_ref, xb_ref, xc_ref, out_ref, held, feats, total, columns, scale, *sums = refs
    sums = (sums[:2], sums[2:])
    blocks_a, _, span = xa_ref.shape
    blocks_b = xb_ref.shape[0] - skip
    groups = span // LANES
    rows_a, rows_b = blocks_a * span, 2 * blocks_b * span
    passes = passes_of(span, blocks_b, skip)
    half = rows_a // 2
    steps = half // step
    lane = lax.broadcasted_iota(jnp.int32, (1, LANES), 1)

    def fill_a(block, carry):
        for group in range(groups):
            points = xa_ref[block, :, group * LANES : (group + 1) * LANES].astype(jnp.float32)
            rest = jnp.zeros((LANES - FPAD, LANES), jnp.float32)
            turned = jnp.concatenate([widened(points, True), rest], axis=0).T.astype(jnp.bfloat16)
            at = pl.ds(pl.multiple_of(block * span + group * LANES, LANES), LANES)
            feats[at, :] = turned
            held[at, :LANES] = turned
            held[at, LANES:] = jnp.zeros((LANES, LANES), jnp.bfloat16)
            total[at, :] = jnp.zeros((LANES, LANES), jnp.float32)
        return carry

    lax.fori_loop(0, blocks_a, fill_a, 0)
    columns[:, :LANES] = jnp.zeros((columns.shape[0], LANES), jnp.float32)
    past = columns.shape[1] - LANES - rows_b
    columns[:, LANES + rows_b :] = jnp.zeros((columns.shape[0], past), jnp.float32)

    def fill_b(block, carry):
        for place, ref in ((block, xb_ref), (blocks_b + block, xc_ref)):
            at = pl.ds(pl.multiple_of(LANES + place * span, LANES), span)
            source = lax.rem(own_ref[0] + 1 + block, blocks_b + 1) if skip else block
            panel = ref[source].astype(jnp.float32)
            columns[:FPAD, at] = widened(panel[:FEAT], False)
            columns[FPAD:, at] = panel[FEAT:]
        return carry

    lax.fori_loop(0, blocks_b, fill_b, 0)
    if skip:
        left = 2 * span % CHUNK
        panel = near_ref[:, span - LANES :].astype(jnp.float32)
        panel = jnp.concatenate([widened(panel[:FEAT], False), panel[FEAT:]], axis=0)
        at = slice(LANES + rows_b, 2 * LANES + rows_b)
        columns[:, at] = jnp.where(lane < left, pltpu.roll(panel, left, 1), 0.0)

    def window(number, low, high):
        start = LANES - FPAD + number * CHUNK
        base = pl.multiple_of((start // LANES) * LANES, LANES)
        shift = start % LANES
        parts = [
            pltpu.roll(columns[low:high, pl.ds(base + k * LANES, LANES)], (LANES - shift) % LANES, 1)
            for k in range(3)
        ]
        keep = lane < LANES - shift
        return jnp.where(keep, parts[0], parts[1]), jnp.where(keep, parts[1], parts[2])

    def stage(number):
        feat_0, feat_1 = window(jnp.minimum(number, passes), 0, FPAD)
        live = jnp.where(number < passes, 1.0, 0.0)
        feat_0 = jnp.where(lane < FPAD, 0.0, feat_0) * live
        dirs_0, dirs_1 = window(jnp.maximum(number - 1, 0), FPAD, FPAD + RIDGE)
        has = jnp.where(number > 0, 1.0, 0.0)
        rest = jnp.zeros((LANES - RIDGE, LANES), jnp.float32)
        turned_0 = jnp.concatenate([dirs_0 * has, rest], axis=0).T
        turned_1 = jnp.concatenate([dirs_1 * has, rest], axis=0).T
        left = jnp.concatenate([feat_0, turned_0[FPAD:], turned_1], axis=0)
        right = jnp.concatenate([feat_1 * live, jnp.zeros((CHUNK, LANES), jnp.float32)], axis=0)
        block = jnp.concatenate([left, right], axis=1).astype(jnp.bfloat16)
        pltpu.matmul_push_rhs(block, 0, 0)
        pltpu.matmul_push_rhs(block, 0, 1)

    scale[...] = jnp.full(scale.shape, LOG2E, jnp.float32)
    to_base_2 = scale[0:1, :]
    keep_feats = lax.broadcasted_iota(jnp.int32, (step, LANES), 1) < FPAD

    def issue(unit, number, fresh):
        at = unit * half + number * step
        pltpu.matmul_acc_lhs(sums[unit][number % 2], held[at : at + step, :], load_staged_rhs=0 if fresh else None)

    def finish(unit, number, last):
        at = unit * half + number * step
        found = pltpu.matmul_pop(sums[unit][number % 2])
        total[at : at + step, :] += found[:, :LANES]
        if not last:
            weights = jnp.exp2(found * to_base_2).astype(jnp.bfloat16)
            held[at : at + step, :LANES] = jnp.where(keep_feats, feats[at : at + step, :], weights[:, :LANES])
            held[at : at + step, LANES:] = weights[:, LANES:]

    def one_pass(more, last):
        for number in range(steps):
            for unit in range(2):
                if number + 1 < steps:
                    issue(unit, number + 1, False)
                elif more:
                    issue(unit, 0, True)
                finish(unit, number, last)

    stage(0)
    for unit in range(2):
        issue(unit, 0, True)
    stage(1)

    def middle(trip, carry):
        for turn in range(TURNS):
            one_pass(True, False)
            stage(trip * TURNS + turn + 2)
        return carry

    trips = (passes - 1) // TURNS
    lax.fori_loop(0, trips, middle, 0)
    for number in range(trips * TURNS, passes - 1):
        one_pass(True, False)
        stage(number + 2)
    one_pass(True, False)
    one_pass(False, True)
    for block in range(blocks_a):
        for group in range(groups):
            at = block * span + group * LANES
            lanes = slice(group * LANES, (group + 1) * LANES)
            found = total[at : at + LANES, :].T[:RIDGE]
            out_ref[block, :, lanes] = found + before_ref[block, :, lanes] if skip else found


def passes_of(span, blocks_b, skip):
    if not skip:
        return 2 * blocks_b * span // CHUNK
    return -(-(2 * blocks_b * span + 2 * span % CHUNK) // CHUNK)


def apply_kernel(rows_of, columns_of, more_columns, own=None, before=None, near=None):
    skip = own is not None
    blocks_a, _, span = rows_of.shape
    blocks_b = columns_of.shape[0] - skip
    rows_a, rows_b = blocks_a * span, 2 * blocks_b * span
    passes = passes_of(span, blocks_b, skip)
    width = LANES + -(-(passes * CHUNK + 2 * WIDE) // LANES) * LANES
    whole = pl.BlockSpec(memory_space=pltpu.VMEM)
    return pl.pallas_call(
        functools.partial(apply_body, skip),
        out_shape=jax.ShapeDtypeStruct((blocks_a, RIDGE, span), jnp.float32),
        in_specs=[pl.BlockSpec(memory_space=pltpu.SMEM), whole, whole] * skip + [whole] * 3,
        scratch_shapes=[
            pltpu.VMEM((rows_a, WIDE), jnp.bfloat16),
            pltpu.VMEM((rows_a, LANES), jnp.bfloat16),
            pltpu.VMEM((rows_a, LANES), jnp.float32),
            pltpu.VMEM((FPAD + RIDGE, width), jnp.float32),
            pltpu.VMEM((8, WIDE), jnp.float32),
        ],
        compiler_params=pltpu.CompilerParams(vmem_limit_bytes=40 * 2**20),
        cost_estimate=pl.CostEstimate(
            flops=2 * rows_a * passes * WIDE * WIDE, bytes_accessed=3 * 2**20, transcendentals=rows_a * rows_b
        ),
        name="kernel_rows_rest" if skip else "kernel_rows",
    )(*([own, before, near] if skip else []), rows_of, columns_of, more_columns)


def rows_body(points_ref, to_rows_ref):
    points = points_ref[...]
    for device in range(to_rows_ref.shape[0]):
        to_rows_ref[device] = points


def place_body(ids_ref, points_ref, dirs_ref, ridge_ref, place_ref, copy_ref, ridged_ref, own_ref, to_pairs_ref):
    ids = ids_ref[...]
    samples = ids.shape[1]
    named = ids.astype(jnp.float32)
    rank = jnp.zeros((1, samples), jnp.int32)
    here = lax.broadcasted_iota(jnp.int32, (LANES, samples), 1)
    for group in range(samples // LANES):
        at = slice(group * LANES, (group + 1) * LANES)
        turned = jnp.broadcast_to(named[:, at], (LANES, LANES)).T
        before = lax.broadcasted_iota(jnp.int32, (LANES, samples), 0) + group * LANES < here
        same = (jnp.concatenate([turned] * (samples // LANES), axis=1) == named) & before
        rank += jnp.sum(jnp.where(same, 1, 0), axis=0, keepdims=True)
    place_ref[...] = (ids // FOLD_DEV) * SPOTS + (ids % FOLD_DEV) * SLOTS + rank
    dirs = dirs_ref[...]
    square = (RIDGE, RIDGE)
    diagonal = lax.broadcasted_iota(jnp.int32, square, 0) == lax.broadcasted_iota(jnp.int32, square, 1)
    copy_ref[...] = dirs
    ridged_ref[...] = jnp.sum(jnp.where(diagonal, ridge_ref[...], 0.0), axis=1, keepdims=True) * dirs
    panel = jnp.concatenate([points_ref[...], dirs.astype(jnp.bfloat16)], axis=0)
    own_ref[0] = panel
    for device in range(to_pairs_ref.shape[0]):
        to_pairs_ref[device] = panel


def scatter_body(devices, shares_ref, dirs_ref, ridged_ref, place_ref, image_ref, send_ref):
    samples = dirs_ref.shape[1]
    dirs = dirs_ref[...]
    image = jnp.sum(shares_ref[...], axis=0) + ridged_ref[...]
    image_ref[...] = image
    pieces = thirds(jnp.concatenate([dirs, image], axis=0))
    rest = jnp.zeros((LANES - 6 * RIDGE, samples), jnp.float32)
    stacked = jnp.concatenate([*pieces, rest], axis=0)
    turned = [stacked[:, group * LANES : (group + 1) * LANES].T for group in range(samples // LANES)]
    turned = jnp.concatenate(turned, axis=0).astype(jnp.bfloat16)
    spot = place_ref[...] - SPOTS * lax.broadcasted_iota(jnp.int32, (devices, samples), 0)
    for quad in range(FOLD_DEV * SLOTS // 4):
        found = []
        for slot in range(4 * quad, 4 * quad + 4):
            chosen = jnp.where(spot == slot, 1.0, 0.0).astype(jnp.bfloat16)
            parts = jnp.dot(chosen, turned, preferred_element_type=jnp.float32)
            found.append(parts[:, :32] + parts[:, 32:64] + parts[:, 64:96])
        send_ref[:, 0, quad * LANES : (quad + 1) * LANES] = jnp.concatenate(found, axis=1)


def fold_body(scale, rows_ref, out_ref):
    rows = rows_ref[:, 0, :]
    width = 2 * RIDGE
    turned = rows.T
    dirs = jnp.concatenate([turned[at : at + RIDGE] for at in range(0, turned.shape[0], width)], axis=0)
    products = jnp.dot(dirs, rows, precision=lax.Precision.HIGHEST, preferred_element_type=jnp.float32)
    for fold in range(FOLD_DEV):
        found = jnp.zeros((RIDGE, RIDGE), jnp.float32)
        for slot in range(fold * SLOTS, (fold + 1) * SLOTS):
            at = width * slot + RIDGE
            found += products[slot * RIDGE : (slot + 1) * RIDGE, at : at + RIDGE]
        lines = [found[line : line + 1, :] for line in range(RIDGE)]
        out_ref[fold : fold + 1, :] = jnp.concatenate(lines, axis=1) * scale


def body(observation_points, search_vectors, shrinkage_levels, holdout_group):
    samples = observation_points.shape[0]
    blk_count, row_count = lax.axis_size("blk"), lax.axis_size("rows")
    devices = blk_count * row_count
    pairs = blk_count // 2
    swap = [(place, place ^ 1) for place in range(blk_count)]
    dirs = search_vectors.T
    points = observation_points.T
    to_rows = pl.pallas_call(
        rows_body, out_shape=jax.ShapeDtypeStruct((row_count, FEAT, samples), jnp.bfloat16), name="rows_to_send"
    )(points)
    rows_of = lax.all_to_all(to_rows, "rows", 0, 0, tiled=True)
    panel_shape = (FEAT + RIDGE, samples)
    place, dirs, ridged, own_panel, to_pairs = pl.pallas_call(
        place_body,
        out_shape=[
            pltpu.VMEM((1, samples), jnp.int32),
            pltpu.VMEM(dirs.shape, jnp.float32),
            pltpu.VMEM(dirs.shape, jnp.float32),
            pltpu.VMEM((1, *panel_shape), jnp.bfloat16),
            jax.ShapeDtypeStruct((pairs, *panel_shape), jnp.bfloat16),
        ],
        name="places",
    )(holdout_group.T, points, dirs, shrinkage_levels[None])
    partner = lax.ppermute(own_panel, "blk", swap)
    rows_of, to_pairs, own_panel, place, dirs, ridged = lax.optimization_barrier(
        (rows_of, to_pairs, own_panel, place, dirs, ridged)
    )
    columns_of = lax.all_to_all(
        to_pairs,
        "blk",
        0,
        0,
        tiled=True,
        axis_index_groups=[[2 * pair + core for pair in range(pairs)] for core in range(2)],
    )
    near = apply_kernel(rows_of, own_panel, partner)
    near, columns_of = lax.optimization_barrier((near, columns_of))
    more_columns = lax.ppermute(columns_of, "blk", swap)
    own = (lax.axis_index("blk") // 2).astype(jnp.int32)[None]
    shares = apply_kernel(rows_of, columns_of, more_columns, own, near, partner[0])
    shares = lax.all_to_all(shares, "rows", 0, 0, tiled=True)
    image, send = pl.pallas_call(
        functools.partial(scatter_body, devices),
        out_shape=[
            jax.ShapeDtypeStruct((RIDGE, samples), jnp.float32),
            jax.ShapeDtypeStruct((devices, 1, 2 * RIDGE * FOLD_DEV * SLOTS), jnp.float32),
        ],
        compiler_params=pltpu.CompilerParams(vmem_limit_bytes=40 * 2**20),
        name="image_and_slots",
    )(shares, dirs, ridged, place)
    received = lax.all_to_all(send, ("blk", "rows"), 0, 0, tiled=True)
    folds = pl.pallas_call(
        functools.partial(fold_body, FOLD_DEV / samples),
        out_shape=jax.ShapeDtypeStruct((FOLD_DEV, RIDGE * RIDGE), jnp.float32),
        compiler_params=pltpu.CompilerParams(vmem_limit_bytes=40 * 2**20),
        name="fold_products",
    )(received)
    return image.T, folds


def solution(mesh):
    split = P(("blk", "rows"), None)
    return jax.shard_map(
        body,
        mesh=mesh,
        in_specs=(split, split, P(), split),
        out_specs=(split, split),
        check_vma=False,
    )
```
